32 devices in a mesh: parts: 2 (over y), tm: 4 (over z), factor: 4 (over x, core).
Axes of the slice: x: 2, y: 2, z: 4, core: 2. Of those that a mesh axis runs over, the one named last changes fastest.
Arguments:
- schur_matrix: float32 [24576, 24, 4, 128], P(('parts', 'tm'), None, 'factor'), parts along dimension 0, as said below
- link_rhs: float32 [24576], P(('parts', 'tm')), parts along dimension 0, may hold values from -6 to 6
- hour_rhs: float32 [32, 256], P(('parts', 'tm', 'factor')), parts along dimension 0, may hold values from -6 to 6
- link_cols: int32 [32, 256], P(('parts', 'tm', 'factor')), parts along dimension 0, may hold values from 0 to 255
- link_coef: float32 [32, 256], P(('parts', 'tm', 'factor')), parts along dimension 0, may hold values from -6 to 6
- hour_inverse: float32 [32, 256, 256], P(('parts', 'tm', 'factor')), parts along dimension 0, may hold values from -0.375 to 0.375
- couple_prev: float32 [32, 2, 256], P(('parts', 'tm', 'factor')), parts along dimension 0, may hold values from -1.2 to 1.2
- couple_next: float32 [32, 2, 256], P(('parts', 'tm', 'factor')), parts along dimension 0, may hold values from -1.2 to 1.2
Outputs:
- schur_trail: float32 [24576, 24, 4, 128], P(('parts', 'tm'), None, 'factor'), parts along dimension 0
- link_trail: float32 [24576], P(('parts', 'tm')), parts along dimension 0
- hour_step: float32 [32, 256], P(('parts', 'tm', 'factor')), parts along dimension 0
The draws below stay inside these ranges and needn't reach their ends.
There are 2 independent parts, one for each index of `parts`. The reference program is written for one: setup_inputs(seed, part) draws one part's arguments, and reference() takes and returns one part's arrays. A program takes and returns all parts, laid end to end along the dimension named above; each array names one. Nothing has to cross between parts.
Inputs may be any that keep to these rules, and one draw needn't show every extreme that they name: schur_matrix is symmetric and its leading 2 * 128 rows and columns form a positive definite block.
All inputs are finite; a program needn't handle non-finite values.
Results may differ from the reference program's by a relative error of at most 0.0001.
Values sent between devices are 32-bit elements; how exact they have to be, the bound alone decides.
A program may use at most 192 MiB of HBM per device.

```python
import math
import jax
import jax.numpy as jnp
from jax import lax

L = 12288
P_SIZE = 128
PANELS = 2
HB = 256
BW = 2
SWEEPS = 2
HOURS = 16
N_FACTOR = 4


def draw_schur_matrix(key, part):
    first_key, second_key = jax.random.split(jax.random.fold_in(key, 11))
    noise = jax.random.uniform(first_key, (L, L), jnp.float32, -1.0, 1.0)
    offdiag = (noise + noise.T) * (1.0 / math.sqrt(L))
    diag_vals = jax.random.uniform(second_key, (L,), jnp.float32, 1.0, 3.0) + PANELS * P_SIZE * 2.0 / math.sqrt(L)
    eye_mat = jnp.eye(L, dtype=jnp.float32)
    whole = offdiag * (1.0 - eye_mat) + eye_mat * diag_vals[:, None]
    return whole.reshape(L, L // (P_SIZE * N_FACTOR), N_FACTOR, P_SIZE)


def set_ends(drawn, own_key, least, largest):
    longest = drawn.shape.index(max(drawn.shape))
    spots = []
    for shift in (0, 1):
        where = [jax.random.randint(jax.random.fold_in(own_key, axis), (), 0, length) for axis, length in enumerate(drawn.shape)]
        where[longest] = (where[longest] + shift) % drawn.shape[longest]
        spots.append(tuple(where))
    return drawn.at[spots[0]].set(least).at[spots[1]].set(largest)


def steps_of(rng, extent, cuts, low, top_value):
    level, own = 1.0, jax.random.fold_in(rng, 6)
    for position, shards_of in cuts:
        draws = jnp.exp(jax.random.uniform(jax.random.fold_in(own, position), (shards_of,), jnp.float32, low / len(cuts), top_value / len(cuts)))
        level = level * jnp.repeat(draws, extent[position] // shards_of).reshape([-1 if axis == position else 1 for axis in range(len(extent))])
    return level


def gaussian(rng, dims, deviation, most, cuts=(), kind=jnp.bfloat16):
    array = deviation * jax.random.normal(rng, dims, jnp.float32)
    if cuts:
        array = array * steps_of(rng, dims, cuts, -0.22, 0.18)
    return jnp.clip(array, -most, most).astype(kind)


def setup_inputs(seed: int = 0, part: int = 0) -> dict:
    seeds = jax.random.split(jax.random.key(seed), 9)
    part_keys = jax.random.split(jax.random.fold_in(seeds[8], part), 9)
    return {
        "schur_matrix": draw_schur_matrix(jax.random.fold_in(jax.random.fold_in(seeds[8], part), 71), part),
        "link_rhs": gaussian(part_keys[1], (L,), 1.0, 6.0, ((0, 4),), jnp.float32),
        "hour_rhs": gaussian(part_keys[2], (HOURS, HB), 1.0, 6.0, ((0, 16),), jnp.float32),
        "link_cols": set_ends(jax.random.randint(part_keys[3], (HOURS, HB), 0, PANELS * P_SIZE), jax.random.fold_in(part_keys[3], 1), 0, (PANELS * P_SIZE) - 1).astype(jnp.int32),
        "link_coef": gaussian(part_keys[4], (HOURS, HB), 1.0, 6.0, ((0, 16),), jnp.float32),
        "hour_inverse": gaussian(part_keys[5], (HOURS, HB, HB), HB ** -0.5, 0.375, ((0, 16),), jnp.float32),
        "couple_prev": gaussian(part_keys[6], (HOURS, BW, HB), 0.2, 1.2, ((0, 16),), jnp.float32),
        "couple_next": gaussian(part_keys[7], (HOURS, BW, HB), 0.2, 1.2, ((0, 16),), jnp.float32),
    }


def reference(schur_matrix, link_rhs, hour_rhs, link_cols, link_coef, hour_inverse, couple_prev, couple_next):
    schur_now = schur_matrix.reshape(L, L)
    rhs_now = link_rhs
    all_rows = jnp.arange(L, dtype=jnp.int32)
    solved = []
    for panel_id in range(PANELS):
        panel_first = panel_id * P_SIZE
        panel_cols = schur_now[:, panel_first:panel_first + P_SIZE]
        diag_block = panel_cols[panel_first:panel_first + P_SIZE]
        lower_block = jnp.linalg.cholesky(diag_block)
        factor_rows = jax.scipy.linalg.solve_triangular(lower_block, panel_cols.T, lower=True).T
        factor_rows = jnp.where((all_rows < panel_first)[:, None], jnp.zeros_like(factor_rows), factor_rows)
        link_step = jax.scipy.linalg.solve_triangular(lower_block, rhs_now[panel_first:panel_first + P_SIZE], lower=True)
        rhs_now = rhs_now - jnp.dot(factor_rows, link_step, precision=lax.Precision.HIGHEST)
        schur_now = schur_now - jnp.dot(factor_rows, factor_rows.T, precision=lax.Precision.HIGHEST)
        solved.append(link_step)
    link_values = jnp.concatenate(solved)
    one_hot = (link_cols[:, :, None] == jnp.arange(PANELS * P_SIZE, dtype=jnp.int32)[None, None, :]).astype(jnp.float32)
    looked = jnp.einsum('hik,k->hi', one_hot, link_values, precision=lax.Precision.HIGHEST)
    target = hour_rhs - link_coef * looked
    hour_state = jnp.einsum('hik,hk->hi', hour_inverse, target, precision=lax.Precision.HIGHEST)
    for sweep_id in range(SWEEPS):
        zero_rows = jnp.zeros((1, BW), jnp.float32)
        prev_last = jnp.concatenate((zero_rows, hour_state[:-1, -BW:]), axis=0)
        next_first = jnp.concatenate((hour_state[1:, :BW], zero_rows), axis=0)
        coupling = jnp.einsum('hbi,hb->hi', couple_prev, prev_last, precision=lax.Precision.HIGHEST)
        coupling = coupling + jnp.einsum('hbi,hb->hi', couple_next, next_first, precision=lax.Precision.HIGHEST)
        hour_state = jnp.einsum('hik,hk->hi', hour_inverse, target - coupling, precision=lax.Precision.HIGHEST)
    return (schur_now.reshape(schur_matrix.shape), rhs_now, hour_state)
```

```python
import functools

import jax
import jax.numpy as jnp
from jax import lax
from jax.experimental import pallas as pl
from jax.experimental.pallas import tpu as pltpu
from jax.sharding import PartitionSpec as P

PANELS = 2
BW = 2
SWEEPS = 2


def spread(array, axis, root):
    mine = lax.axis_index(axis) == root
    return lax.psum(jnp.where(mine, array, jnp.zeros_like(array)), axis)


def with_halo(cells, sides, width):
    for axis, dim in sides:
        count = lax.axis_size(axis)
        ends = count - 1
        head = lax.slice_in_dim(cells, 0, width, axis=dim)
        tail = lax.slice_in_dim(cells, cells.shape[dim] - width, cells.shape[dim], axis=dim)
        cells = jnp.concatenate(
            [
                lax.ppermute(tail, axis, [(i, (i + 1) % count) for i in range(ends)]),
                cells,
                lax.ppermute(head, axis, [((i + 1) % count, i) for i in range(ends)]),
            ],
            axis=dim,
        )
    return cells


def comm_kernel(nz, ms, parts_k, own, rhs, CR, CC, D, RS, lsem, xs, xr, cs, cr, ds, dr, fs, fr, bs, br):
    f = lax.axis_index("factor")
    z = lax.axis_index("tm")
    p = lax.rem(f, 2)
    q = 1 - p
    xx = lax.div(f, 2)
    mate = f + 1 - 2 * p
    over = f + 2 - 4 * xx
    per = ms // parts_k
    chunks = [(0, 1, 0, 2)] + [(k * per, (k + 1) * per, 2, 4) for k in range(parts_k)] + [(1, ms, 0, 2)]
    last = len(chunks) - 1

    def piece(panel, j):
        a, b, c, d = chunks[j]
        return CR.at[panel, a:b, c:d]

    def xcopy(j):
        return pltpu.make_async_remote_copy(
            src_ref=piece(p, j), dst_ref=piece(p, j), send_sem=xs.at[j], recv_sem=xr.at[j],
            device_id={"factor": over}, device_id_type=pl.DeviceIdType.MESH)

    def ccopy(j, panel):
        return pltpu.make_async_remote_copy(
            src_ref=piece(panel, j), dst_ref=piece(panel, j), send_sem=cs.at[j], recv_sem=cr.at[j],
            device_id={"factor": mate}, device_id_type=pl.DeviceIdType.MESH)

    def zcopy(owner, d, k, step, send, recv):
        spot = CC.at[:, pl.ds(owner * ms + k * per, per)]
        src = CR.at[:, k * per:(k + 1) * per, f] if d == 0 else spot
        return pltpu.make_async_remote_copy(
            src_ref=src, dst_ref=spot, send_sem=send.at[d, k], recv_sem=recv.at[d, k],
            device_id={"tm": z + step}, device_id_type=pl.DeviceIdType.MESH)

    def fwd(d, k):
        return zcopy(z - d, d, k, 1, fs, fr)

    def bwd(d, k):
        return zcopy(z + d, d, k, -1, bs, br)

    def fwd_in(d, k):
        return pltpu.make_async_remote_copy(
            src_ref=CC.at[:, pl.ds((z - 1 - d) * ms + k * per, per)],
            dst_ref=CC.at[:, pl.ds((z - 1 - d) * ms + k * per, per)],
            send_sem=fs.at[d, k], recv_sem=fr.at[d, k],
            device_id={"tm": z - 1}, device_id_type=pl.DeviceIdType.MESH)

    def bwd_in(d, k):
        return pltpu.make_async_remote_copy(
            src_ref=CC.at[:, pl.ds((z + 1 + d) * ms + k * per, per)],
            dst_ref=CC.at[:, pl.ds((z + 1 + d) * ms + k * per, per)],
            send_sem=bs.at[d, k], recv_sem=br.at[d, k],
            device_id={"tm": z + 1}, device_id_type=pl.DeviceIdType.MESH)

    def dcopies():
        return [
            pltpu.make_async_remote_copy(
                src_ref=ref, dst_ref=ref, send_sem=ds.at[i], recv_sem=dr.at[i],
                device_id={"tm": z + 1}, device_id_type=pl.DeviceIdType.MESH)
            for i, ref in enumerate((D, RS))]

    barrier = pltpu.get_barrier_semaphore()
    pl.semaphore_signal(barrier, inc=1, device_id={"factor": mate}, device_id_type=pl.DeviceIdType.MESH)
    pl.semaphore_signal(barrier, inc=1, device_id={"factor": over}, device_id_type=pl.DeviceIdType.MESH)

    @pl.when(z > 0)
    def _():
        pl.semaphore_signal(barrier, inc=1, device_id={"tm": z - 1}, device_id_type=pl.DeviceIdType.MESH)

    @pl.when(z < nz - 1)
    def _():
        pl.semaphore_signal(barrier, inc=1, device_id={"tm": z + 1}, device_id_type=pl.DeviceIdType.MESH)

    pl.semaphore_wait(barrier, 2 + jnp.where(z > 0, 1, 0) + jnp.where(z < nz - 1, 1, 0))

    def own_sends(k):
        @pl.when(z < nz - 1)
        def _():
            fwd(0, k).start()

        @pl.when(z > 0)
        def _():
            bwd(0, k).start()

    def diag_send():
        @pl.when(z == 0)
        def _():
            one = pltpu.make_async_copy(CR.at[:, 0, 0:2], D, lsem.at[1])
            two = pltpu.make_async_copy(rhs.at[0:8], RS, lsem.at[2])
            one.start()
            two.start()
            one.wait()
            two.wait()
            if nz > 1:
                for c in dcopies():
                    c.start()

    @pl.when(xx == 0)
    def _():
        mine = pltpu.make_async_copy(own, CR.at[p], lsem.at[0])
        mine.start()
        mine.wait()
        for j in range(last + 1):
            ccopy(j, p).start()
            xcopy(j).start()
        ccopy(0, q).wait_recv()
        diag_send()
        for j in range(1, last + 1):
            ccopy(j, q).wait_recv()
        for k in range(parts_k):
            own_sends(k)

    @pl.when(xx == 1)
    def _():
        xcopy(0).wait_recv()
        ccopy(0, p).start()
        ccopy(0, q).wait_recv()
        diag_send()
        for k in range(parts_k):
            xcopy(k + 1).wait_recv()
            ccopy(k + 1, p).start()
            ccopy(k + 1, q).wait_recv()
            own_sends(k)

    local = pltpu.make_async_copy(CR.at[:, :, f], CC.at[:, pl.ds(z * ms, ms)], lsem.at[3])
    local.start()

    @pl.when(z > 0)
    def _():
        pair = dcopies()
        for c in pair:
            c.wait_recv()

        @pl.when(z < nz - 1)
        def _():
            for c in pair:
                c.start()

    for s in range(nz - 1):
        for k in range(parts_k):
            @pl.when(z - 1 - s >= 0)
            def _():
                fwd_in(s, k).wait_recv()
                if s + 1 < nz - 1:
                    @pl.when(z < nz - 1)
                    def _():
                        fwd(s + 1, k).start()

            @pl.when(z + 1 + s < nz)
            def _():
                bwd_in(s, k).wait_recv()
                if s + 1 < nz - 1:
                    @pl.when(z > 0)
                    def _():
                        bwd(s + 1, k).start()

        if s == 0:
            @pl.when(xx == 1)
            def _():
                xcopy(last).wait_recv()
                ccopy(last, p).start()
                ccopy(last, q).wait_recv()

    for j in range(last + 1):
        ccopy(j, p).wait_send()

        @pl.when(xx == 0)
        def _():
            xcopy(j).wait_send()

    @pl.when(z < nz - 1)
    def _():
        for c in dcopies():
            c.wait_send()

    for d in range(nz - 1):
        for k in range(parts_k):
            @pl.when((z < nz - 1) & (z - d >= 0))
            def _():
                fwd(d, k).wait_send()

            @pl.when((z > 0) & (z + d < nz))
            def _():
                bwd(d, k).wait_send()

    local.wait()


def gather_columns(own, rhs, nz):
    ms = own.shape[0]
    w = own.shape[3]
    parts_k = 3 if ms % 3 == 0 else 1
    n = parts_k + 2
    hops = max(nz - 1, 1)
    dma = pltpu.SemaphoreType.DMA
    anyspace = pl.BlockSpec(memory_space=pl.ANY)
    return pl.pallas_call(
        functools.partial(comm_kernel, nz, ms, parts_k),
        out_shape=(
            jax.ShapeDtypeStruct((2, ms, 4, w, w), jnp.float32),
            jax.ShapeDtypeStruct((2, nz * ms, w, w), jnp.float32),
            jax.ShapeDtypeStruct((2, 2, w, w), jnp.float32),
            jax.ShapeDtypeStruct((8, w), jnp.float32),
        ),
        in_specs=[anyspace, anyspace],
        out_specs=(anyspace,) * 4,
        scratch_shapes=[
            dma((4,)), dma((n,)), dma((n,)), dma((n,)), dma((n,)), dma((2,)), dma((2,)),
            dma((hops, parts_k)), dma((hops, parts_k)), dma((hops, parts_k)), dma((hops, parts_k)),
        ],
        compiler_params=pltpu.CompilerParams(collective_id=0, has_side_effects=True),
    )(own, rhs)


def split(a):
    high = a.astype(jnp.bfloat16)
    return high, (a - high.astype(jnp.float32)).astype(jnp.bfloat16)


def update_kernel(tiles, rows, s_ref, f_ref, g_ref, o_ref, gh_ref, gl_ref):
    w = s_ref.shape[1]

    @pl.when(pl.program_id(0) == 0)
    def _():
        for t in range(0, tiles, 2):
            at = slice(t * w, (t + 2) * w)
            gh_ref[:, at], gl_ref[:, at] = split(g_ref[:, at])

    fh, fl = split(f_ref[...])
    for t in range(0, tiles, 2):
        gh = gh_ref[:, t * w:(t + 2) * w]
        gl = gl_ref[:, t * w:(t + 2) * w]
        upd = jnp.dot(fh, gh, preferred_element_type=jnp.float32)
        upd = upd + jnp.dot(fh, gl, preferred_element_type=jnp.float32)
        upd = upd + jnp.dot(fl, gh, preferred_element_type=jnp.float32)
        for i in range(2):
            at = pl.ds(t + i, rows, stride=tiles)
            o_ref[at, :] = s_ref[at, :] - upd[:, i * w:(i + 1) * w]


def update(flat, frow, fcol, tiles):
    rows_here, depth = frow.shape
    w = flat.shape[1]
    rows = 128
    return pl.pallas_call(
        functools.partial(update_kernel, tiles, rows),
        grid=(rows_here // rows,),
        out_shape=jax.ShapeDtypeStruct(flat.shape, jnp.float32),
        in_specs=[
            pl.BlockSpec((rows * tiles, w), lambda i: (i, 0)),
            pl.BlockSpec((rows, depth), lambda i: (i, 0)),
            pl.BlockSpec(fcol.shape, lambda i: (0, 0)),
        ],
        out_specs=pl.BlockSpec((rows * tiles, w), lambda i: (i, 0)),
        scratch_shapes=[pltpu.VMEM(fcol.shape, jnp.bfloat16), pltpu.VMEM(fcol.shape, jnp.bfloat16)],
        compiler_params=pltpu.CompilerParams(vmem_limit_bytes=40 * 1024 * 1024),
        cost_estimate=pl.CostEstimate(
            flops=6 * rows_here * tiles * w * depth, bytes_accessed=8 * flat.size, transcendentals=0),
    )(flat, frow, fcol)


def eliminate(schur, rhs):
    rows_here, tiles, _, w = schur.shape
    nz = lax.axis_size("tm")
    z = lax.axis_index("tm")
    f = lax.axis_index("factor")
    own = schur[:, 0, 0, :].reshape(rows_here // (4 * w), 4, w, w)
    cr, cc, d, rs = gather_columns(own, rhs.reshape(-1, w), nz)
    diag = jnp.transpose(d, (1, 2, 0, 3)).reshape(2 * w, 2 * w)
    lower = jnp.linalg.cholesky(diag)
    inv = jax.scipy.linalg.solve_triangular(lower, jnp.eye(2 * w, dtype=jnp.float32), lower=True)
    inv = jnp.tril(inv)
    hp = lax.Precision.HIGHEST
    link = jnp.dot(inv, rs[:2].reshape(-1), precision=hp)
    inv0, inv1 = inv[:, :w], inv[:, w:]
    c0, c1 = cr.reshape(2, rows_here, w)
    frow = jnp.dot(c0, inv0.T, precision=hp) + jnp.dot(c1, inv1.T, precision=hp)
    grow = z * rows_here + jnp.arange(rows_here, dtype=jnp.int32)
    late = jnp.arange(2 * w, dtype=jnp.int32) >= w
    frow = jnp.where((grow < w)[:, None] & late[None, :], 0.0, frow)
    k0, k1 = cc.reshape(2, tiles * w, w)
    fcol = jnp.dot(inv0, k0.T, precision=hp) + jnp.dot(inv1, k1.T, precision=hp)
    first = (jnp.arange(tiles * w, dtype=jnp.int32) < w) & (f == 0)
    fcol = jnp.where(late[:, None] & first[None, :], 0.0, fcol)
    trail = rhs - jnp.dot(frow, link, precision=hp)
    out = update(schur.reshape(rows_here * tiles, w), frow, fcol, tiles)
    return out.reshape(schur.shape), trail, link


def panels_by_step(schur_now, rhs_now):
    rows_here = schur_now.shape[0]
    tiles_here = schur_now.shape[1]
    width = schur_now.shape[3]
    factors = lax.axis_size("factor")
    row_start = lax.axis_index("tm") * rows_here
    global_rows = row_start + jnp.arange(rows_here, dtype=jnp.int32)
    factor_here = lax.axis_index("factor")
    solved = []
    for panel_id in range(PANELS):
        column_tile = panel_id // factors
        owner_index = panel_id % factors
        own_cols = schur_now[:, column_tile, 0, :]
        panel_cols = spread(own_cols, "factor", owner_index)
        panel_first = panel_id * width
        picker = (
            global_rows[:, None] - panel_first == jnp.arange(width, dtype=jnp.int32)[None, :]
        ).astype(jnp.float32)
        block_part = jnp.dot(picker.T, panel_cols, precision=lax.Precision.HIGHEST)
        rhs_part = jnp.dot(picker.T, rhs_now, precision=lax.Precision.HIGHEST)
        diag_block, rhs_segment = lax.psum((block_part, rhs_part), "tm")
        lower_block = jnp.linalg.cholesky(diag_block)
        factor_rows = jax.scipy.linalg.solve_triangular(lower_block, panel_cols.T, lower=True).T
        factor_rows = jnp.where(
            (global_rows < panel_first)[:, None], jnp.zeros_like(factor_rows), factor_rows
        )
        all_factor = lax.all_gather(factor_rows, "tm", axis=0, tiled=True)
        grouped = all_factor.reshape(tiles_here, factors, width, width)
        my_tiles = lax.dynamic_index_in_dim(grouped, factor_here, 1, keepdims=False)
        link_step = jax.scipy.linalg.solve_triangular(lower_block, rhs_segment, lower=True)
        rhs_now = rhs_now - jnp.dot(factor_rows, link_step, precision=lax.Precision.HIGHEST)
        update = jnp.einsum("rk,tck->rtc", factor_rows, my_tiles, precision=lax.Precision.HIGHEST)
        schur_now = schur_now - update[:, :, None, :]
        solved.append(link_step)
    return schur_now, rhs_now, jnp.concatenate(solved)


def shards(
    schur_matrix, link_rhs, hour_rhs, link_cols, link_coef, hour_inverse, couple_prev, couple_next
):
    rows_here = schur_matrix.shape[0]
    width = schur_matrix.shape[3]
    factors = lax.axis_size("factor")
    wide = factors == 4 and rows_here % (factors * width) == 0
    wide = wide and rows_here >= 2 * factors * width and schur_matrix.shape[1] % 8 == 0
    step = eliminate if wide else panels_by_step
    schur_now, rhs_now, link_values = step(schur_matrix, link_rhs)
    one_hot = (
        link_cols[:, :, None] == jnp.arange(PANELS * width, dtype=jnp.int32)[None, None, :]
    ).astype(jnp.float32)
    looked = jnp.einsum("hik,k->hi", one_hot, link_values, precision=lax.Precision.HIGHEST)
    target = hour_rhs - link_coef * looked
    hour_state = jnp.einsum("hik,hk->hi", hour_inverse, target, precision=lax.Precision.HIGHEST)
    for sweep_id in range(SWEEPS):
        border_pairs = jnp.concatenate((hour_state[:, :BW], hour_state[:, -BW:]), axis=1)
        padded = with_halo(border_pairs, ((("tm", "factor"), 0),), 1)
        prev_last = padded[:-2, BW:]
        next_first = padded[2:, :BW]
        coupling = jnp.einsum("hbi,hb->hi", couple_prev, prev_last, precision=lax.Precision.HIGHEST)
        coupling = coupling + jnp.einsum(
            "hbi,hb->hi", couple_next, next_first, precision=lax.Precision.HIGHEST
        )
        hour_state = jnp.einsum(
            "hik,hk->hi", hour_inverse, target - coupling, precision=lax.Precision.HIGHEST
        )
    return (schur_now, rhs_now, hour_state)


def solution(mesh):
    placed = (
        P(("parts", "tm"), None, "factor", None),
        P(("parts", "tm")),
        P(("parts", "tm", "factor"), None),
        P(("parts", "tm", "factor"), None),
        P(("parts", "tm", "factor"), None),
        P(("parts", "tm", "factor"), None, None),
        P(("parts", "tm", "factor"), None, None),
        P(("parts", "tm", "factor"), None, None),
    )
    return jax.shard_map(
        shards,
        mesh=mesh,
        in_specs=placed,
        out_specs=(
            P(("parts", "tm"), None, "factor", None),
            P(("parts", "tm")),
            P(("parts", "tm", "factor"), None),
        ),
        check_vma=False,
    )
```

```python
import functools

import jax
import jax.numpy as jnp
from jax import lax
from jax.experimental import pallas as pl
from jax.experimental.pallas import tpu as pltpu
from jax.sharding import PartitionSpec as P

PANELS = 2
BW = 2
SWEEPS = 2


def spread(array, axis, root):
    mine = lax.axis_index(axis) == root
    return lax.psum(jnp.where(mine, array, jnp.zeros_like(array)), axis)


def with_halo(cells, sides, width):
    for axis, dim in sides:
        count = lax.axis_size(axis)
        ends = count - 1
        head = lax.slice_in_dim(cells, 0, width, axis=dim)
        tail = lax.slice_in_dim(cells, cells.shape[dim] - width, cells.shape[dim], axis=dim)
        cells = jnp.concatenate(
            [
                lax.ppermute(tail, axis, [(i, (i + 1) % count) for i in range(ends)]),
                cells,
                lax.ppermute(head, axis, [((i + 1) % count, i) for i in range(ends)]),
            ],
            axis=dim,
        )
    return cells


def comm_kernel(nz, ms, parts_k, own, rhs, CR, CC, D, RS, lsem, xs, xr, cs, cr, ds, dr, fs, fr, bs, br):
    f = lax.axis_index("factor")
    z = lax.axis_index("tm")
    p = lax.rem(f, 2)
    q = 1 - p
    xx = lax.div(f, 2)
    mate = f + 1 - 2 * p
    over = f + 2 - 4 * xx
    per = ms // parts_k
    chunks = [(0, 1, 0, 2)] + [(k * per, (k + 1) * per, 2, 4) for k in range(parts_k)] + [(1, ms, 0, 2)]
    last = len(chunks) - 1

    def piece(panel, j):
        a, b, c, d = chunks[j]
        return CR.at[panel, a:b, c:d]

    def xcopy(j):
        return pltpu.make_async_remote_copy(
            src_ref=piece(p, j), dst_ref=piece(p, j), send_sem=xs.at[j], recv_sem=xr.at[j],
            device_id={"factor": over}, device_id_type=pl.DeviceIdType.MESH)

    def ccopy(j, panel):
        return pltpu.make_async_remote_copy(
            src_ref=piece(panel, j), dst_ref=piece(panel, j), send_sem=cs.at[j], recv_sem=cr.at[j],
            device_id={"factor": mate}, device_id_type=pl.DeviceIdType.MESH)

    def zcopy(owner, d, k, step, send, recv):
        spot = CC.at[:, pl.ds(owner * ms + k * per, per)]
        src = CR.at[:, k * per:(k + 1) * per, f] if d == 0 else spot
        return pltpu.make_async_remote_copy(
            src_ref=src, dst_ref=spot, send_sem=send.at[d, k], recv_sem=recv.at[d, k],
            device_id={"tm": z + step}, device_id_type=pl.DeviceIdType.MESH)

    def fwd(d, k):
        return zcopy(z - d, d, k, 1, fs, fr)

    def bwd(d, k):
        return zcopy(z + d, d, k, -1, bs, br)

    def fwd_in(d, k):
        return pltpu.make_async_remote_copy(
            src_ref=CC.at[:, pl.ds((z - 1 - d) * ms + k * per, per)],
            dst_ref=CC.at[:, pl.ds((z - 1 - d) * ms + k * per, per)],
            send_sem=fs.at[d, k], recv_sem=fr.at[d, k],
            device_id={"tm": z - 1}, device_id_type=pl.DeviceIdType.MESH)

    def bwd_in(d, k):
        return pltpu.make_async_remote_copy(
            src_ref=CC.at[:, pl.ds((z + 1 + d) * ms + k * per, per)],
            dst_ref=CC.at[:, pl.ds((z + 1 + d) * ms + k * per, per)],
            send_sem=bs.at[d, k], recv_sem=br.at[d, k],
            device_id={"tm": z + 1}, device_id_type=pl.DeviceIdType.MESH)

    def dcopies():
        return [
            pltpu.make_async_remote_copy(
                src_ref=ref, dst_ref=ref, send_sem=ds.at[i], recv_sem=dr.at[i],
                device_id={"tm": z + 1}, device_id_type=pl.DeviceIdType.MESH)
            for i, ref in enumerate((D, RS))]

    barrier = pltpu.get_barrier_semaphore()
    pl.semaphore_signal(barrier, inc=1, device_id={"factor": mate}, device_id_type=pl.DeviceIdType.MESH)
    pl.semaphore_signal(barrier, inc=1, device_id={"factor": over}, device_id_type=pl.DeviceIdType.MESH)

    @pl.when(z > 0)
    def _():
        pl.semaphore_signal(barrier, inc=1, device_id={"tm": z - 1}, device_id_type=pl.DeviceIdType.MESH)

    @pl.when(z < nz - 1)
    def _():
        pl.semaphore_signal(barrier, inc=1, device_id={"tm": z + 1}, device_id_type=pl.DeviceIdType.MESH)

    pl.semaphore_wait(barrier, 2 + jnp.where(z > 0, 1, 0) + jnp.where(z < nz - 1, 1, 0))

    def own_sends(k):
        @pl.when(z < nz - 1)
        def _():
            fwd(0, k).start()

        @pl.when(z > 0)
        def _():
            bwd(0, k).start()

    def diag_send():
        @pl.when(z == 0)
        def _():
            one = pltpu.make_async_copy(CR.at[:, 0, 0:2], D, lsem.at[1])
            two = pltpu.make_async_copy(rhs.at[0:8], RS, lsem.at[2])
            one.start()
            two.start()
            one.wait()
            two.wait()
            if nz > 1:
                for c in dcopies():
                    c.start()

    @pl.when(xx == 0)
    def _():
        mine = pltpu.make_async_copy(own, CR.at[p], lsem.at[0])
        mine.start()
        mine.wait()
        for j in range(last + 1):
            ccopy(j, p).start()
            xcopy(j).start()
        ccopy(0, q).wait_recv()
        diag_send()
        for j in range(1, last + 1):
            ccopy(j, q).wait_recv()
        for k in range(parts_k):
            own_sends(k)

    @pl.when(xx == 1)
    def _():
        xcopy(0).wait_recv()
        ccopy(0, p).start()
        ccopy(0, q).wait_recv()
        diag_send()
        for k in range(parts_k):
            xcopy(k + 1).wait_recv()
            ccopy(k + 1, p).start()
            ccopy(k + 1, q).wait_recv()
            own_sends(k)

    local = pltpu.make_async_copy(CR.at[:, :, f], CC.at[:, pl.ds(z * ms, ms)], lsem.at[3])
    local.start()

    @pl.when(z > 0)
    def _():
        pair = dcopies()
        for c in pair:
            c.wait_recv()

        @pl.when(z < nz - 1)
        def _():
            for c in pair:
                c.start()

    for s in range(nz - 1):
        for k in range(parts_k):
            @pl.when(z - 1 - s >= 0)
            def _():
                fwd_in(s, k).wait_recv()
                if s + 1 < nz - 1:
                    @pl.when(z < nz - 1)
                    def _():
                        fwd(s + 1, k).start()

            @pl.when(z + 1 + s < nz)
            def _():
                bwd_in(s, k).wait_recv()
                if s + 1 < nz - 1:
                    @pl.when(z > 0)
                    def _():
                        bwd(s + 1, k).start()

        if s == 0:
            @pl.when(xx == 1)
            def _():
                xcopy(last).wait_recv()
                ccopy(last, p).start()
                ccopy(last, q).wait_recv()

    for j in range(last + 1):
        ccopy(j, p).wait_send()

        @pl.when(xx == 0)
        def _():
            xcopy(j).wait_send()

    @pl.when(z < nz - 1)
    def _():
        for c in dcopies():
            c.wait_send()

    for d in range(nz - 1):
        for k in range(parts_k):
            @pl.when((z < nz - 1) & (z - d >= 0))
            def _():
                fwd(d, k).wait_send()

            @pl.when((z > 0) & (z + d < nz))
            def _():
                bwd(d, k).wait_send()

    local.wait()


def gather_columns(own, rhs, nz):
    ms = own.shape[0]
    w = own.shape[3]
    parts_k = 3 if ms % 3 == 0 else 1
    n = parts_k + 2
    hops = max(nz - 1, 1)
    dma = pltpu.SemaphoreType.DMA
    anyspace = pl.BlockSpec(memory_space=pl.ANY)
    return pl.pallas_call(
        functools.partial(comm_kernel, nz, ms, parts_k),
        out_shape=(
            jax.ShapeDtypeStruct((2, ms, 4, w, w), jnp.float32),
            jax.ShapeDtypeStruct((2, nz * ms, w, w), jnp.float32),
            jax.ShapeDtypeStruct((2, 2, w, w), jnp.float32),
            jax.ShapeDtypeStruct((8, w), jnp.float32),
        ),
        in_specs=[anyspace, anyspace],
        out_specs=(anyspace,) * 4,
        scratch_shapes=[
            dma((4,)), dma((n,)), dma((n,)), dma((n,)), dma((n,)), dma((2,)), dma((2,)),
            dma((hops, parts_k)), dma((hops, parts_k)), dma((hops, parts_k)), dma((hops, parts_k)),
        ],
        compiler_params=pltpu.CompilerParams(collective_id=0, has_side_effects=True),
    )(own, rhs)


def split(a):
    high = a.astype(jnp.bfloat16)
    return high, (a - high.astype(jnp.float32)).astype(jnp.bfloat16)


HIGH = lax.Precision.HIGHEST


def across(a, b):
    return lax.dot_general(
        a, b, (((1,), (1,)), ((), ())), precision=HIGH, preferred_element_type=jnp.float32)


def update_kernel(tiles, rows, rows_here, s_ref, c_ref, k_ref, inv_ref, o_ref, g_ref):
    w = s_ref.shape[1]
    step = pl.program_id(0)
    inv0 = inv_ref[:, :w]
    inv1 = inv_ref[:, w:]

    @pl.when(step == 0)
    def _():
        owner = lax.axis_index("factor") == 0
        out = lax.broadcasted_iota(jnp.int32, (2 * w, 2 * w), 0)
        col = lax.broadcasted_iota(jnp.int32, (2 * w, 2 * w), 1)
        for t in range(0, tiles, 2):
            at = slice(t * w, (t + 2) * w)
            g = across(inv0, k_ref[0, at, :]) + across(inv1, k_ref[1, at, :])
            if t == 0:
                limit = jnp.where(owner, w, 0)
                g = jnp.where((out >= w) & (col < limit), 0.0, g)
            gh, gl = split(g)
            g_ref[:2 * w, at] = gh
            g_ref[2 * w:4 * w, at] = gl
            g_ref[4 * w:, at] = gh

    first = lax.axis_index("tm") * rows_here + step * rows
    frow = across(c_ref[0], inv0) + across(c_ref[1], inv1)
    row = lax.broadcasted_iota(jnp.int32, frow.shape, 0) + first
    depth = lax.broadcasted_iota(jnp.int32, frow.shape, 1)
    fh, fl = split(jnp.where((row < w) & (depth >= w), 0.0, frow))
    left = jnp.concatenate([fh, fh, fl], axis=1)
    for t in range(0, tiles, 2):
        upd = jnp.dot(left, g_ref[:, t * w:(t + 2) * w], preferred_element_type=jnp.float32)
        for i in range(2):
            at = pl.ds(t + i, rows, stride=tiles)
            o_ref[at, :] = s_ref[at, :] - upd[:, i * w:(i + 1) * w]


def update(flat, crow, ccol, inv, tiles):
    rows_here = crow.shape[1]
    w = flat.shape[1]
    rows = 2 * w
    return pl.pallas_call(
        functools.partial(update_kernel, tiles, rows, rows_here),
        grid=(rows_here // rows,),
        out_shape=jax.ShapeDtypeStruct(flat.shape, jnp.float32),
        in_specs=[
            pl.BlockSpec((rows * tiles, w), lambda i: (i, 0)),
            pl.BlockSpec((2, rows, w), lambda i: (0, i, 0)),
            pl.BlockSpec(ccol.shape, lambda i: (0, 0, 0)),
            pl.BlockSpec(inv.shape, lambda i: (0, 0)),
        ],
        out_specs=pl.BlockSpec((rows * tiles, w), lambda i: (i, 0)),
        scratch_shapes=[pltpu.VMEM((6 * w, tiles * w), jnp.bfloat16)],
        compiler_params=pltpu.CompilerParams(vmem_limit_bytes=48 * 1024 * 1024),
        cost_estimate=pl.CostEstimate(
            flops=12 * rows_here * tiles * w * w, bytes_accessed=8 * flat.size, transcendentals=0),
    )(flat, crow, ccol, inv)


def lower_inverse(block):
    eye = jnp.eye(block.shape[0], dtype=jnp.float32)
    return jnp.tril(jax.scipy.linalg.solve_triangular(jnp.linalg.cholesky(block), eye, lower=True))


def eliminate(schur, rhs):
    rows_here, tiles, _, w = schur.shape
    nz = lax.axis_size("tm")
    z = lax.axis_index("tm")
    own = schur[:, 0, 0, :].reshape(rows_here // (4 * w), 4, w, w)
    cr, cc, d, rs = gather_columns(own, rhs.reshape(-1, w), nz)
    top = lower_inverse(d[0, 0])
    side = jnp.dot(d[0, 1], top.T, precision=HIGH)
    low = lower_inverse(d[1, 1] - jnp.dot(side, side.T, precision=HIGH))
    mixed = -jnp.dot(low, jnp.dot(side, top, precision=HIGH), precision=HIGH)
    zero = jnp.zeros((w, w), jnp.float32)
    inv = jnp.concatenate(
        [jnp.concatenate([top, zero], axis=1), jnp.concatenate([mixed, low], axis=1)], axis=0)
    link = jnp.dot(inv, rs[:2].reshape(-1), precision=HIGH)
    crow = cr.reshape(2, rows_here, w)
    out = update(schur.reshape(rows_here * tiles, w), crow, cc.reshape(2, tiles * w, w), inv, tiles)
    back = jnp.dot(link, inv, precision=HIGH)
    early = jnp.dot(link[:w], top, precision=HIGH)
    both = jnp.dot(jnp.stack([back[:w], early]), crow[0].T, precision=HIGH)
    rest = jnp.dot(crow[1], back[w:], precision=HIGH)
    grow = z * rows_here + jnp.arange(rows_here, dtype=jnp.int32)
    trail = rhs - jnp.where(grow < w, both[1], both[0] + rest)
    return out.reshape(schur.shape), trail, link


def panels_by_step(schur_now, rhs_now):
    rows_here = schur_now.shape[0]
    tiles_here = schur_now.shape[1]
    width = schur_now.shape[3]
    factors = lax.axis_size("factor")
    row_start = lax.axis_index("tm") * rows_here
    global_rows = row_start + jnp.arange(rows_here, dtype=jnp.int32)
    factor_here = lax.axis_index("factor")
    solved = []
    for panel_id in range(PANELS):
        column_tile = panel_id // factors
        owner_index = panel_id % factors
        own_cols = schur_now[:, column_tile, 0, :]
        panel_cols = spread(own_cols, "factor", owner_index)
        panel_first = panel_id * width
        picker = (
            global_rows[:, None] - panel_first == jnp.arange(width, dtype=jnp.int32)[None, :]
        ).astype(jnp.float32)
        block_part = jnp.dot(picker.T, panel_cols, precision=lax.Precision.HIGHEST)
        rhs_part = jnp.dot(picker.T, rhs_now, precision=lax.Precision.HIGHEST)
        diag_block, rhs_segment = lax.psum((block_part, rhs_part), "tm")
        lower_block = jnp.linalg.cholesky(diag_block)
        factor_rows = jax.scipy.linalg.solve_triangular(lower_block, panel_cols.T, lower=True).T
        factor_rows = jnp.where(
            (global_rows < panel_first)[:, None], jnp.zeros_like(factor_rows), factor_rows
        )
        all_factor = lax.all_gather(factor_rows, "tm", axis=0, tiled=True)
        grouped = all_factor.reshape(tiles_here, factors, width, width)
        my_tiles = lax.dynamic_index_in_dim(grouped, factor_here, 1, keepdims=False)
        link_step = jax.scipy.linalg.solve_triangular(lower_block, rhs_segment, lower=True)
        rhs_now = rhs_now - jnp.dot(factor_rows, link_step, precision=lax.Precision.HIGHEST)
        update = jnp.einsum("rk,tck->rtc", factor_rows, my_tiles, precision=lax.Precision.HIGHEST)
        schur_now = schur_now - update[:, :, None, :]
        solved.append(link_step)
    return schur_now, rhs_now, jnp.concatenate(solved)


def shards(
    schur_matrix, link_rhs, hour_rhs, link_cols, link_coef, hour_inverse, couple_prev, couple_next
):
    rows_here = schur_matrix.shape[0]
    width = schur_matrix.shape[3]
    factors = lax.axis_size("factor")
    wide = factors == 4 and rows_here % (factors * width) == 0
    wide = wide and rows_here >= 2 * factors * width and schur_matrix.shape[1] % 8 == 0
    step = eliminate if wide else panels_by_step
    schur_now, rhs_now, link_values = step(schur_matrix, link_rhs)
    one_hot = (
        link_cols[:, :, None] == jnp.arange(PANELS * width, dtype=jnp.int32)[None, None, :]
    ).astype(jnp.float32)
    looked = jnp.einsum("hik,k->hi", one_hot, link_values, precision=lax.Precision.HIGHEST)
    target = hour_rhs - link_coef * looked
    hour_state = jnp.einsum("hik,hk->hi", hour_inverse, target, precision=lax.Precision.HIGHEST)
    for sweep_id in range(SWEEPS):
        border_pairs = jnp.concatenate((hour_state[:, :BW], hour_state[:, -BW:]), axis=1)
        padded = with_halo(border_pairs, ((("tm", "factor"), 0),), 1)
        prev_last = padded[:-2, BW:]
        next_first = padded[2:, :BW]
        coupling = jnp.einsum("hbi,hb->hi", couple_prev, prev_last, precision=lax.Precision.HIGHEST)
        coupling = coupling + jnp.einsum(
            "hbi,hb->hi", couple_next, next_first, precision=lax.Precision.HIGHEST
        )
        hour_state = jnp.einsum(
            "hik,hk->hi", hour_inverse, target - coupling, precision=lax.Precision.HIGHEST
        )
    return (schur_now, rhs_now, hour_state)


def solution(mesh):
    placed = (
        P(("parts", "tm"), None, "factor", None),
        P(("parts", "tm")),
        P(("parts", "tm", "factor"), None),
        P(("parts", "tm", "factor"), None),
        P(("parts", "tm", "factor"), None),
        P(("parts", "tm", "factor"), None, None),
        P(("parts", "tm", "factor"), None, None),
        P(("parts", "tm", "factor"), None, None),
    )
    return jax.shard_map(
        shards,
        mesh=mesh,
        in_specs=placed,
        out_specs=(
            P(("parts", "tm"), None, "factor", None),
            P(("parts", "tm")),
            P(("parts", "tm", "factor"), None),
        ),
        check_vma=False,
    )
```
